32 devices in a mesh: lat: 16 (over z, y, x), depth: 2 (over core).
Axes of the slice: x: 2, y: 2, z: 4, core: 2. Of those that a mesh axis runs over, the one named last changes fastest.
Arguments:
- saved_waves: float32 [2, 32, 2, 256, 256], P(None, 'lat', 'depth'), may hold values from -5 to 5
- object_slices: float32 [2, 2, 256, 4096], P(None, 'depth', None, 'lat'), may hold values from -5 to 5
- cotangent: float32 [2, 32, 256, 256], P(None, 'lat'), may hold values from -5 to 5
- transfer_phase: float32 [256, 256], replicated, may hold values from -3.140625 to 3.140625
- offsets: int32 [32], P('lat'), may hold values from 0 to 255
Outputs:
- object_grad: float32 [2, 2, 256, 4096], P(None, 'depth', None, 'lat')
- probe_grad: float32 [2, 256, 256], P(None, 'depth')
The draws below stay inside these ranges and needn't reach their ends.
All inputs are finite; a program needn't handle non-finite values.
Results may differ from the reference program's by a relative error of at most 0.0003.
Values sent between devices are 32-bit elements; how exact they have to be, the bound alone decides.
A program may use at most 64 MiB of HBM per device.

```python
import jax
import jax.numpy as jnp
from jax import lax

PW = 256
P_DEV = 2
POS = 32
SLICES = 2
OW = 4096


def set_ends(entries, stream_key, low, top_value):
    longest = entries.shape.index(max(entries.shape))
    spots = []
    for shift in (0, 1):
        where = [jax.random.randint(jax.random.fold_in(stream_key, axis), (), 0, length) for axis, length in enumerate(entries.shape)]
        where[longest] = (where[longest] + shift) % entries.shape[longest]
        spots.append(tuple(where))
    return entries.at[spots[0]].set(low).at[spots[1]].set(top_value)


def level_of(key, dims, shards, smallest, high):
    level, own = 1.0, jax.random.fold_in(key, 6)
    for dim, parts in shards:
        steps = jnp.exp(jax.random.uniform(jax.random.fold_in(own, dim), (parts,), jnp.float32, smallest / len(shards), high / len(shards)))
        level = level * jnp.repeat(steps, dims[dim] // parts).reshape([-1 if axis == dim else 1 for axis in range(len(dims))])
    return level


def scatter_about(key, extent, spread, limit, pieces=(), kind=jnp.bfloat16):
    result = spread * jax.random.normal(key, extent, jnp.float32)
    if pieces:
        result = result * level_of(key, extent, pieces, -0.22, 0.18)
    return jnp.clip(result, -limit, limit).astype(kind)


def setup_inputs(seed: int = 0) -> dict:
    keys = jax.random.split(jax.random.key(seed), 6)
    return {
        "saved_waves": scatter_about(keys[0], (2, POS, SLICES, PW, PW), 0.7, 5.0, ((1, 16), (2, 2)), jnp.float32),
        "object_slices": scatter_about(keys[1], (2, SLICES, PW, OW), 0.7, 5.0, ((1, 2), (3, 16)), jnp.float32),
        "cotangent": scatter_about(keys[2], (2, POS, PW, PW), 0.7, 5.0, ((1, 16),), jnp.float32),
        "transfer_phase": jnp.clip(jax.random.uniform(keys[3], (PW, PW), jnp.float32, -3.140625, 3.140625), -3.140625, 3.140625),
        "offsets": set_ends(jax.random.randint(keys[4], (POS,), 0, PW), jax.random.fold_in(keys[4], 1), 0, PW - 1).astype(jnp.int32),
    }


def reference(saved_waves, object_slices, cotangent, transfer_phase, offsets):
    prop = jnp.exp(1j * transfer_phase)
    obj = object_slices[0] + 1j * object_slices[1]
    waves = saved_waves[0] + 1j * saved_waves[1]
    cotan = cotangent[0] + 1j * cotangent[1]
    position_ids = jnp.arange(POS, dtype=jnp.int32)
    starts = (position_ids // P_DEV) * PW + offsets.astype(jnp.int32)
    column_ids = jnp.arange(PW, dtype=jnp.int32)

    def one_position(carry, index):
        grad_acc, probe_acc = carry
        columns = (starts[index] + column_ids) % OW
        patches = jnp.take(obj, columns, axis=2)
        wave = cotan[index]
        deltas = []
        for layer in reversed(range(SLICES)):
            back = jnp.fft.ifft2(jnp.conj(prop) * jnp.fft.fft2(wave, norm="ortho"), norm="ortho")
            deltas.append(jnp.conj(waves[index, layer]) * back)
            wave = jnp.conj(patches[layer]) * back
        stacked = jnp.stack(deltas[::-1])
        grad_acc = grad_acc.at[:, :, columns].add(stacked)
        return (grad_acc, probe_acc + wave), None

    init = (jnp.zeros_like(obj), jnp.zeros_like(cotan[0]))
    (grad_acc, probe_acc), _ = lax.scan(one_position, init, position_ids)
    object_grad = jnp.stack([jnp.real(grad_acc), jnp.imag(grad_acc)])
    probe_grad = jnp.stack([jnp.real(probe_acc), jnp.imag(probe_acc)])
    return object_grad, probe_grad
```

```python
import functools
import math

import jax
import jax.numpy as jnp
import ml_dtypes
import numpy as np
from jax import lax
from jax.experimental import pallas as pl
from jax.experimental.pallas import tpu as pltpu
from jax.sharding import PartitionSpec as P

F32 = jnp.float32
BF16 = jnp.bfloat16
MESH_ID = pl.DeviceIdType.MESH


def dft_tables(length):
    index = np.arange(length)
    angles = (index[:, None] * index[None, :] % length) * (2.0 * math.pi / length)
    re, im = np.cos(angles) / math.sqrt(length), -np.sin(angles) / math.sqrt(length)
    left = np.block([[re, -im], [im, re]])
    high = left.astype(ml_dtypes.bfloat16)
    low = (left - high.astype(np.float64)).astype(ml_dtypes.bfloat16)
    return np.stack([high, low, high.T, low.T])


def cos_sin(phase):
    half = phase * 0.5
    sq = half * half
    sin_half = half * (1.0 + sq * (-1 / 6 + sq * (1 / 120 + sq * (-1 / 5040 + sq * (1 / 362880 + sq * (-1 / 39916800 + sq * (1 / 6227020800)))))))
    cos_half = 1.0 + sq * (-1 / 2 + sq * (1 / 24 + sq * (-1 / 720 + sq * (1 / 40320 + sq * (-1 / 3628800 + sq * (1 / 479001600 + sq * (-1 / 87178291200)))))))
    return 1.0 - 2.0 * sin_half * sin_half, 2.0 * sin_half * cos_half


def dot(a, b):
    return jnp.dot(a, b, preferred_element_type=F32)


def kernel(
    lat_size, depth_size, reduce_inside,
    obj_hbm, saved_hbm, cot_hbm, phase_hbm, tab_hbm, off_ref,
    grad_ref, probe_ref,
    obj, psi, cot, phase, tab, halo, wave, gout, ah, al, bh, bl, cosr, sinr,
    over, over_in, gsum, band, slots, mine, final,
    lsem, halo_s, halo_r, over_s, over_r, wave_s, wave_r, band_s, band_r, rs_s, rs_r, ag_s, ag_r,
):
    width = obj.shape[2]
    count = psi.shape[1]
    lat = lax.axis_index("lat")
    depth = lax.axis_index("depth")
    left = lax.rem(lat + lat_size - 1, lat_size)
    right = lax.rem(lat + 1, lat_size)
    last = depth == depth_size - 1

    loads = [
        pltpu.make_async_copy(source, target, lsem.at[n])
        for n, (source, target) in enumerate(
            ((phase_hbm, phase), (cot_hbm, cot), (tab_hbm, tab), (saved_hbm, psi), (obj_hbm, obj))
        )
    ]
    for load in loads:
        load.start()

    barrier = pltpu.get_barrier_semaphore()
    for k in range(1, lat_size):
        pl.semaphore_signal(barrier, inc=1, device_id=(lax.rem(lat + k, lat_size), depth), device_id_type=MESH_ID)
    for k in range(1, depth_size):
        pl.semaphore_signal(barrier, inc=1, device_id=(lat, lax.rem(depth + k, depth_size)), device_id_type=MESH_ID)
    pl.semaphore_wait(barrier, lat_size - 1 + depth_size - 1)

    halo_copy = pltpu.make_async_remote_copy(
        src_ref=obj_hbm, dst_ref=halo, send_sem=halo_s, recv_sem=halo_r,
        device_id=(left, depth), device_id_type=MESH_ID,
    )
    halo_copy.start()

    loads[0].wait()
    cosr[...], sinr[...] = cos_sin(phase[...])
    loads[1].wait()

    @pl.when(last)
    def _():
        for p in range(count):
            for c in range(2):
                wave[c, p] = pltpu.roll(cot[c, p], off_ref[p], 1)

    loads[2].wait()
    loads[3].wait()
    for p in range(count):
        for c in range(2):
            psi[c, p, 0] = pltpu.roll(psi[c, p, 0], off_ref[p], 1)

    wave_copy = pltpu.make_async_remote_copy(
        src_ref=gout, dst_ref=wave, send_sem=wave_s, recv_sem=wave_r,
        device_id=(lat, lax.rem(depth + depth_size - 1, depth_size)), device_id_type=MESH_ID,
    )

    @pl.when(depth < depth_size - 1)
    def _():
        wave_copy.wait_recv()

    def put(high_ref, low_ref, row, col, block):
        rows, cols = pl.ds(row * width, width), pl.ds(col * width, width)
        high = block.astype(BF16)
        high_ref[rows, cols] = high
        low_ref[rows, cols] = (block - high.astype(F32)).astype(BF16)

    def block_of(n, size=1):
        return pl.ds(n * width, size * width)

    def left_block(high, low, row, col, src_h, src_l):
        r, c = block_of(row), block_of(col)
        return dot(tab[high, r, :], src_h[:, c]) + (dot(tab[high, r, :], src_l[:, c]) + dot(tab[low, r, :], src_h[:, c]))

    def right_block(high, low, row, col, src_h, src_l):
        r, c = block_of(row), block_of(col)
        return dot(src_h[r, :], tab[high, :, c]) + (dot(src_l[r, :], tab[high, :, c]) + dot(src_h[r, :], tab[low, :, c]))

    for p in range(count):
        for c in range(2):
            put(ah, al, c, p, wave[c, p])
    for p in range(count):
        for c in range(2):
            put(bh, bl, p, c, left_block(0, 1, c, p, ah, al))
    for p in range(count):
        re = right_block(2, 3, p, 0, bh, bl)
        im = right_block(2, 3, p, 1, bh, bl)
        put(bh, bl, p, 0, re * cosr[...] + im * sinr[...])
        put(bh, bl, p, 1, im * cosr[...] - re * sinr[...])
    for p in range(count):
        for c in range(2):
            put(ah, al, c, p, right_block(0, 1, p, c, bh, bl))
    column = lax.broadcasted_iota(jnp.int32, (width, width), 1)
    for p in range(count):
        re = left_block(2, 3, 0, p, ah, al)
        im = left_block(2, 3, 1, p, ah, al)
        wave[0, p] = re
        wave[1, p] = im
        own = column >= off_ref[p]
        saved_re, saved_im = psi[0, p, 0], psi[1, p, 0]
        delta = (saved_re * re + saved_im * im, saved_re * im - saved_im * re)
        for c in range(2):
            if p == 0:
                grad_ref[c, 0] = jnp.where(own, delta[c], 0.0)
                over[c] = jnp.where(own, 0.0, delta[c])
            else:
                grad_ref[c, 0] += jnp.where(own, delta[c], 0.0)
                over[c] += jnp.where(own, 0.0, delta[c])
    over_copy = pltpu.make_async_remote_copy(
        src_ref=over, dst_ref=over_in, send_sem=over_s, recv_sem=over_r,
        device_id=(right, depth), device_id_type=MESH_ID,
    )
    over_copy.start()

    loads[4].wait()
    halo_copy.wait_recv()
    for p in range(count):
        own = column >= off_ref[p]
        trans_re = jnp.where(own, obj[0, 0], halo[0, 0])
        trans_im = jnp.where(own, obj[1, 0], halo[1, 0])
        re, im = wave[0, p], wave[1, p]
        gout[0, p] = trans_re * re + trans_im * im
        gout[1, p] = trans_re * im - trans_im * re

    @pl.when(depth > 0)
    def _():
        wave_copy.start()

    @pl.when(depth == 0)
    def _():
        for c in range(2):
            total = pltpu.roll(gout[c, 0], width - off_ref[0], 1)
            for p in range(1, count):
                total = total + pltpu.roll(gout[c, p], width - off_ref[p], 1)
            gsum[c] = total

    if reduce_inside:
        rows = width // depth_size
        piece = rows // lat_size

        def band_copy(r):
            return pltpu.make_async_remote_copy(
                src_ref=gsum.at[:, pl.ds(r * rows, rows), :], dst_ref=band, send_sem=band_s.at[r], recv_sem=band_r,
                device_id=(lat, r), device_id_type=MESH_ID,
            )

        @pl.when(depth == 0)
        def _():
            for r in range(1, depth_size):
                band_copy(r).start()
            band[...] = gsum[:, :rows, :]

        @pl.when(depth > 0)
        def _():
            band_copy(1).wait_recv()

        def part(n):
            return pl.ds(pl.multiple_of(n * piece, piece), piece)

        scatter, gather = [], []
        for k in range(1, lat_size):
            peer = lax.rem(lat + k, lat_size)
            scatter.append(pltpu.make_async_remote_copy(
                src_ref=band.at[:, part(peer), :], dst_ref=slots.at[k], send_sem=rs_s.at[k], recv_sem=rs_r.at[k],
                device_id=(peer, depth), device_id_type=MESH_ID,
            ))
            gather.append(pltpu.make_async_remote_copy(
                src_ref=mine, dst_ref=final.at[:, part(lat), :], send_sem=ag_s.at[k], recv_sem=ag_r.at[k],
                device_id=(peer, depth), device_id_type=MESH_ID,
            ))
        for copy in scatter:
            copy.start()
        total = band[:, part(lat), :]
        for k, copy in enumerate(scatter):
            copy.wait_recv()
            total = total + slots[k + 1]
        mine[...] = total
        for copy in gather:
            copy.start()
        final[:, part(lat), :] = total

    over_copy.wait_recv()
    grad_ref[:, 0] += over_in[...]

    if reduce_inside:
        for copy in gather:
            copy.wait_recv()
        probe_ref[...] = final[...]
        for copy in scatter + gather:
            copy.wait_send()

        @pl.when(depth == 0)
        def _():
            for r in range(1, depth_size):
                band_copy(r).wait_send()
    else:
        probe_ref[...] = jnp.zeros_like(probe_ref)

        @pl.when(depth == 0)
        def _():
            probe_ref[...] = gsum[...]

    @pl.when(depth > 0)
    def _():
        wave_copy.wait_send()

    halo_copy.wait_send()
    over_copy.wait_send()


def shards(lat_size, depth_size, saved_waves, object_slices, cotangent, transfer_phase, offsets):
    width = object_slices.shape[2]
    count = offsets.shape[0]
    reduce_inside = width % (8 * depth_size * lat_size) == 0
    rows = width // depth_size if reduce_inside else width
    piece = max(8, rows // lat_size)
    tables = jnp.asarray(dft_tables(width))
    anywhere = pl.BlockSpec(memory_space=pl.ANY)
    field = pltpu.VMEM((2, count, width, width), F32)
    plane = pltpu.VMEM((2, width, width), F32)
    a_part = pltpu.VMEM((2 * width, count * width), BF16)
    b_part = pltpu.VMEM((count * width, 2 * width), BF16)
    table = pltpu.VMEM((width, width), F32)
    dma = pltpu.SemaphoreType.DMA
    grad, probe = pl.pallas_call(
        functools.partial(kernel, lat_size, depth_size, reduce_inside),
        out_shape=(
            jax.ShapeDtypeStruct(object_slices.shape, F32),
            jax.ShapeDtypeStruct((2, rows, width), F32),
        ),
        in_specs=[anywhere] * 5 + [pl.BlockSpec(memory_space=pltpu.SMEM)],
        out_specs=(pl.BlockSpec(memory_space=pltpu.VMEM),) * 2,
        scratch_shapes=[
            pltpu.VMEM(object_slices.shape, F32),
            pltpu.VMEM(saved_waves.shape, F32),
            field,
            table,
            pltpu.VMEM(tables.shape, BF16),
            pltpu.VMEM(object_slices.shape, F32),
            field,
            field,
            a_part, a_part, b_part, b_part,
            table, table,
            plane, plane, plane,
            pltpu.VMEM((2, rows, width), F32),
            pltpu.VMEM((lat_size, 2, piece, width), F32),
            pltpu.VMEM((2, piece, width), F32),
            pltpu.VMEM((2, rows, width), F32),
            dma((5,)), dma, dma, dma, dma, dma, dma, dma((depth_size,)), dma,
            dma((lat_size,)), dma((lat_size,)), dma((lat_size,)), dma((lat_size,)),
        ],
        compiler_params=pltpu.CompilerParams(
            collective_id=0, has_side_effects=True, vmem_limit_bytes=40 * 1024 * 1024
        ),
        name="ptycho_backward",
    )(object_slices, saved_waves, cotangent, transfer_phase, tables, offsets)
    if not reduce_inside:
        probe = lax.psum(lax.psum_scatter(probe, "depth", scatter_dimension=1, tiled=True), "lat")
    return grad, probe


def solution(mesh):
    placed = (
        P(None, "lat", "depth", None, None),
        P(None, "depth", None, "lat"),
        P(None, "lat", None, None),
        P(),
        P("lat"),
    )
    return jax.shard_map(
        functools.partial(shards, mesh.shape["lat"], mesh.shape["depth"]),
        mesh=mesh,
        in_specs=placed,
        out_specs=(P(None, "depth", None, "lat"), P(None, "depth", None)),
        check_vma=False,
    )
```

```python
import functools
import math

import jax
import jax.numpy as jnp
import ml_dtypes
import numpy as np
from jax import lax
from jax.experimental import pallas as pl
from jax.experimental.pallas import tpu as pltpu
from jax.sharding import PartitionSpec as P

F32 = jnp.float32
BF16 = jnp.bfloat16
MESH_ID = pl.DeviceIdType.MESH
CHUNKS = 4
SCHEDULE = ((0, 4, 0, 0), (4, 0, 0, 0))


def dft_tables(length):
    index = np.arange(length)
    angles = (index[:, None] * index[None, :] % length) * (2.0 * math.pi / length)
    re, im = np.cos(angles) / math.sqrt(length), -np.sin(angles) / math.sqrt(length)
    left = np.block([[re, -im], [im, re]])
    high = left.astype(ml_dtypes.bfloat16)
    low = (left - high.astype(np.float64)).astype(ml_dtypes.bfloat16)
    return np.stack([high, low, high.T, low.T])


def cos_sin(phase):
    half = phase * 0.5
    sq = half * half
    sin_half = half * (1.0 + sq * (-1 / 6 + sq * (1 / 120 + sq * (-1 / 5040 + sq * (1 / 362880 + sq * (-1 / 39916800 + sq * (1 / 6227020800)))))))
    cos_half = 1.0 + sq * (-1 / 2 + sq * (1 / 24 + sq * (-1 / 720 + sq * (1 / 40320 + sq * (-1 / 3628800 + sq * (1 / 479001600 + sq * (-1 / 87178291200)))))))
    return 1.0 - 2.0 * sin_half * sin_half, 2.0 * sin_half * cos_half


def dot(a, b):
    return jnp.dot(a, b, preferred_element_type=F32)


def kernel(
    lat_size, depth_size, reduce_inside,
    obj_hbm, saved_hbm, cot_hbm, phase_hbm, tab_hbm, off_ref,
    grad_ref, probe_ref,
    obj, psi, cot, phase, tab, halo, wave, gout, ah, al, bh, bl, cosr, sinr,
    over, over_in, gsum, band, slots, mine, paired, total_out, final,
    lsem, halo_s, halo_r, over_s, over_r, wave_s, wave_r, band_s, band_r, rs_s, rs_r, ag_s, ag_r, pair_s, pair_r, halo_go, over_go,
):
    width = obj.shape[2]
    count = psi.shape[1]
    lat = lax.axis_index("lat")
    depth = lax.axis_index("depth")
    left = lax.rem(lat + lat_size - 1, lat_size)
    right = lax.rem(lat + 1, lat_size)
    last = depth == depth_size - 1

    loads = [
        pltpu.make_async_copy(source, target, lsem.at[n])
        for n, (source, target) in enumerate(
            ((phase_hbm, phase), (cot_hbm, cot), (tab_hbm, tab), (saved_hbm, psi), (obj_hbm, obj))
        )
    ]
    for load in loads:
        load.start()

    barrier = pltpu.get_barrier_semaphore()
    for k in range(1, lat_size):
        pl.semaphore_signal(barrier, inc=1, device_id=(lax.rem(lat + k, lat_size), depth), device_id_type=MESH_ID)
    for k in range(1, depth_size):
        pl.semaphore_signal(barrier, inc=1, device_id=(lat, lax.rem(depth + k, depth_size)), device_id_type=MESH_ID)
    pl.semaphore_wait(barrier, lat_size - 1 + depth_size - 1)

    halo_copy = pltpu.make_async_remote_copy(
        src_ref=obj_hbm, dst_ref=halo, send_sem=halo_s, recv_sem=halo_r,
        device_id=(left, depth), device_id_type=MESH_ID,
    )

    @pl.when(last)
    def _():
        halo_copy.start()

    loads[0].wait()
    cosr[...], sinr[...] = cos_sin(phase[...])
    loads[1].wait()

    @pl.when(last)
    def _():
        for p in range(count):
            for c in range(2):
                wave[c, p] = pltpu.roll(cot[c, p], off_ref[p], 1)

    loads[2].wait()
    loads[3].wait()
    for p in range(count):
        for c in range(2):
            psi[c, p, 0] = pltpu.roll(psi[c, p, 0], off_ref[p], 1)

    wave_copies = [
        pltpu.make_async_remote_copy(
            src_ref=gout.at[:, p], dst_ref=wave.at[:, p], send_sem=wave_s.at[p], recv_sem=wave_r.at[p],
            device_id=(lat, lax.rem(depth + depth_size - 1, depth_size)), device_id_type=MESH_ID,
        )
        for p in range(count)
    ]

    above, below = (lat, lax.rem(depth + 1, depth_size)), (lat, lax.rem(depth + depth_size - 1, depth_size))

    @pl.when(depth < depth_size - 1)
    def _():
        pl.semaphore_wait(halo_go, 1)
        halo_copy.start()
        halo_copy.wait_send()
        pl.semaphore_signal(over_go, inc=1, device_id=above, device_id_type=MESH_ID)

        @pl.when(depth > 0)
        def _():
            pl.semaphore_signal(halo_go, inc=1, device_id=below, device_id_type=MESH_ID)

    def put(high_ref, low_ref, row, col, block):
        rows, cols = pl.ds(row * width, width), pl.ds(col * width, width)
        high = block.astype(BF16)
        high_ref[rows, cols] = high
        low_ref[rows, cols] = (block - high.astype(F32)).astype(BF16)

    def block_of(n, size=1):
        return pl.ds(n * width, size * width)

    def left_block(high, low, row, col, src_h, src_l):
        r, c = block_of(row), block_of(col)
        return dot(tab[high, r, :], src_h[:, c]) + (dot(tab[high, r, :], src_l[:, c]) + dot(tab[low, r, :], src_h[:, c]))

    def right_block(high, low, row, col, src_h, src_l):
        r, c = block_of(row), block_of(col)
        return dot(src_h[r, :], tab[high, :, c]) + (dot(src_l[r, :], tab[high, :, c]) + dot(src_h[r, :], tab[low, :, c]))

    column = lax.broadcasted_iota(jnp.int32, (width, width), 1)
    for p in range(count):
        @pl.when(depth < depth_size - 1)
        def _(p=p):
            wave_copies[p].wait_recv()

        for c in range(2):
            put(ah, al, c, p, wave[c, p])
        for c in range(2):
            put(bh, bl, p, c, left_block(0, 1, c, p, ah, al))
        re = right_block(2, 3, p, 0, bh, bl)
        im = right_block(2, 3, p, 1, bh, bl)
        put(bh, bl, p, 0, re * cosr[...] + im * sinr[...])
        put(bh, bl, p, 1, im * cosr[...] - re * sinr[...])
        for c in range(2):
            put(ah, al, c, p, right_block(0, 1, p, c, bh, bl))
        re = left_block(2, 3, 0, p, ah, al)
        im = left_block(2, 3, 1, p, ah, al)
        wave[0, p] = re
        wave[1, p] = im
        own = column >= off_ref[p]
        saved_re, saved_im = psi[0, p, 0], psi[1, p, 0]
        delta = (saved_re * re + saved_im * im, saved_re * im - saved_im * re)
        for c in range(2):
            if p == 0:
                grad_ref[c, 0] = jnp.where(own, delta[c], 0.0)
                over[c] = jnp.where(own, 0.0, delta[c])
            else:
                grad_ref[c, 0] += jnp.where(own, delta[c], 0.0)
                over[c] += jnp.where(own, 0.0, delta[c])
    chunk = width // CHUNKS
    over_copies = [
        pltpu.make_async_remote_copy(
            src_ref=over.at[:, pl.ds(n * chunk, chunk), :], dst_ref=over_in.at[:, pl.ds(n * chunk, chunk), :],
            send_sem=over_s.at[n], recv_sem=over_r.at[n], device_id=(right, depth), device_id_type=MESH_ID,
        )
        for n in range(CHUNKS)
    ]
    plan = SCHEDULE if reduce_inside else ((CHUNKS, 0, 0, 0),) * 2

    def send_over(point, front):
        first = sum(plan[1 - front][:point])
        for copy in over_copies[first:first + plan[1 - front][point]]:
            copy.start()

    def send_over_both(point):
        @pl.when(depth == 0)
        def _():
            send_over(point, 1)

        @pl.when(depth > 0)
        def _():
            send_over(point, 0)

    @pl.when(depth == 0)
    def _():
        send_over(0, 1)

    @pl.when(last)
    def _():
        halo_copy.wait_send()
        if depth_size > 1:
            pl.semaphore_signal(halo_go, inc=1, device_id=below, device_id_type=MESH_ID)

    loads[4].wait()
    halo_copy.wait_recv()
    for p in range(count):
        own = column >= off_ref[p]
        trans_re = jnp.where(own, obj[0, 0], halo[0, 0])
        trans_im = jnp.where(own, obj[1, 0], halo[1, 0])
        re, im = wave[0, p], wave[1, p]
        gout[0, p] = trans_re * re + trans_im * im
        gout[1, p] = trans_re * im - trans_im * re

        @pl.when(depth > 0)
        def _(p=p):
            wave_copies[p].start()

    @pl.when(depth > 0)
    def _():
        pl.semaphore_wait(over_go, 1)
        send_over(0, 0)

    @pl.when(depth == 0)
    def _():
        for c in range(2):
            total = pltpu.roll(gout[c, 0], width - off_ref[0], 1)
            for p in range(1, count):
                total = total + pltpu.roll(gout[c, p], width - off_ref[p], 1)
            gsum[c] = total

    if reduce_inside:
        rows = width // depth_size
        lanes = lat_size // 2
        piece = rows // lanes

        def band_copy(r):
            return pltpu.make_async_remote_copy(
                src_ref=gsum.at[:, pl.ds(r * rows, rows), :], dst_ref=band, send_sem=band_s.at[r], recv_sem=band_r,
                device_id=(lat, r), device_id_type=MESH_ID,
            )

        @pl.when(depth == 0)
        def _():
            for r in range(1, depth_size):
                band_copy(r).start()
            band[...] = gsum[:, :rows, :]

        @pl.when(depth > 0)
        def _():
            band_copy(1).wait_recv()

        def part(n):
            return pl.ds(pl.multiple_of(n * piece, piece), piece)

        rank, parity = lat // 2, lax.rem(lat, 2)
        pair = pltpu.make_async_remote_copy(
            src_ref=mine, dst_ref=paired, send_sem=pair_s, recv_sem=pair_r,
            device_id=(lat + 1 - 2 * parity, depth), device_id_type=MESH_ID,
        )
        scatter, gather = [], []
        for k in range(1, lanes):
            slot = lax.rem(rank + k, lanes)
            peer = 2 * slot + parity
            scatter.append(pltpu.make_async_remote_copy(
                src_ref=band.at[:, part(slot), :], dst_ref=slots.at[k], send_sem=rs_s.at[k], recv_sem=rs_r.at[k],
                device_id=(peer, depth), device_id_type=MESH_ID,
            ))
            gather.append(pltpu.make_async_remote_copy(
                src_ref=total_out, dst_ref=final.at[:, part(rank), :], send_sem=ag_s.at[k], recv_sem=ag_r.at[k],
                device_id=(peer, depth), device_id_type=MESH_ID,
            ))
        for copy in scatter:
            copy.start()
        send_over_both(1)
        total = band[:, part(rank), :]
        for k, copy in enumerate(scatter):
            copy.wait_recv()
            total = total + slots[k + 1]
        mine[...] = total
        pair.start()
        send_over_both(2)
        pair.wait_recv()
        total = total + paired[...]
        total_out[...] = total
        for copy in gather:
            copy.start()
        send_over_both(3)
        final[:, part(rank), :] = total

    for n, copy in enumerate(over_copies):
        copy.wait_recv()
        grad_ref[:, 0, n * chunk:(n + 1) * chunk, :] += over_in[:, n * chunk:(n + 1) * chunk, :]

    if reduce_inside:
        for copy in gather:
            copy.wait_recv()
        probe_ref[...] = final[...]
        for copy in scatter + gather + [pair]:
            copy.wait_send()

        @pl.when(depth == 0)
        def _():
            for r in range(1, depth_size):
                band_copy(r).wait_send()
    else:
        probe_ref[...] = jnp.zeros_like(probe_ref)

        @pl.when(depth == 0)
        def _():
            probe_ref[...] = gsum[...]

    @pl.when(depth > 0)
    def _():
        for copy in wave_copies:
            copy.wait_send()

    for copy in over_copies:
        copy.wait_send()


def shards(lat_size, depth_size, saved_waves, object_slices, cotangent, transfer_phase, offsets):
    width = object_slices.shape[2]
    count = offsets.shape[0]
    reduce_inside = lat_size % 2 == 0 and width % (4 * depth_size * lat_size) == 0
    rows = width // depth_size if reduce_inside else width
    piece = max(8, 2 * rows // lat_size)
    tables = jnp.asarray(dft_tables(width))
    anywhere = pl.BlockSpec(memory_space=pl.ANY)
    field = pltpu.VMEM((2, count, width, width), F32)
    plane = pltpu.VMEM((2, width, width), F32)
    a_part = pltpu.VMEM((2 * width, count * width), BF16)
    b_part = pltpu.VMEM((count * width, 2 * width), BF16)
    table = pltpu.VMEM((width, width), F32)
    dma = pltpu.SemaphoreType.DMA
    grad, probe = pl.pallas_call(
        functools.partial(kernel, lat_size, depth_size, reduce_inside),
        out_shape=(
            jax.ShapeDtypeStruct(object_slices.shape, F32),
            jax.ShapeDtypeStruct((2, rows, width), F32),
        ),
        in_specs=[anywhere] * 5 + [pl.BlockSpec(memory_space=pltpu.SMEM)],
        out_specs=(pl.BlockSpec(memory_space=pltpu.VMEM),) * 2,
        scratch_shapes=[
            pltpu.VMEM(object_slices.shape, F32),
            pltpu.VMEM(saved_waves.shape, F32),
            field,
            table,
            pltpu.VMEM(tables.shape, BF16),
            pltpu.VMEM(object_slices.shape, F32),
            field,
            field,
            a_part, a_part, b_part, b_part,
            table, table,
            plane, plane, plane,
            pltpu.VMEM((2, rows, width), F32),
            pltpu.VMEM((lat_size, 2, piece, width), F32),
            pltpu.VMEM((2, piece, width), F32),
            pltpu.VMEM((2, piece, width), F32),
            pltpu.VMEM((2, piece, width), F32),
            pltpu.VMEM((2, rows, width), F32),
            dma((5,)), dma, dma, dma((CHUNKS,)), dma((CHUNKS,)), dma((count,)), dma((count,)), dma((depth_size,)), dma,
            dma((lat_size,)), dma((lat_size,)), dma((lat_size,)), dma((lat_size,)), dma, dma,
            pltpu.SemaphoreType.REGULAR, pltpu.SemaphoreType.REGULAR,
        ],
        compiler_params=pltpu.CompilerParams(
            collective_id=0, has_side_effects=True, vmem_limit_bytes=60 * 1024 * 1024
        ),
        name="ptycho_backward",
    )(object_slices, saved_waves, cotangent, transfer_phase, tables, offsets)
    if not reduce_inside:
        probe = lax.psum(lax.psum_scatter(probe, "depth", scatter_dimension=1, tiled=True), "lat")
    return grad, probe


def solution(mesh):
    placed = (
        P(None, "lat", "depth", None, None),
        P(None, "depth", None, "lat"),
        P(None, "lat", None, None),
        P(),
        P("lat"),
    )
    return jax.shard_map(
        functools.partial(shards, mesh.shape["lat"], mesh.shape["depth"]),
        mesh=mesh,
        in_specs=placed,
        out_specs=(P(None, "depth", None, "lat"), P(None, "depth", None)),
        check_vma=False,
    )
```
